32 devices in a mesh: seq: 16 (over z, y, core), kv: 2 (over x).
Axes of the slice: x: 2, y: 2, z: 4, core: 2. Of those that a mesh axis runs over, the one named last changes fastest.
Arguments:
- queries: bfloat16 [4096, 32, 128], P('seq', 'kv'), may hold values from -6 to 6
- keys: bfloat16 [4096, 16, 128], P('seq', 'kv'), may hold values from -6 to 6
- values: bfloat16 [4096, 16, 128], P('seq', 'kv'), may hold values from -6 to 6
- output_gradient: bfloat16 [4096, 32, 128], P('seq', 'kv'), may hold values from -288 to 288
- window_start: int32 [4096], P('seq'), may hold values from 0 to 4095, as said below
- query_gain: float32 [128], replicated, may hold values from 0.1 to 1.9
- key_gain: float32 [128], replicated, may hold values from 0.1 to 1.9
Outputs:
- query_grad: bfloat16 [4096, 32, 128], P('seq', 'kv')
- key_grad: bfloat16 [4096, 16, 128], P('seq', 'kv')
- value_grad: bfloat16 [4096, 16, 128], P('seq', 'kv')
- query_gain_grad: float32 [128], replicated
- key_gain_grad: float32 [128], replicated
The draws below stay inside these ranges and needn't reach their ends.
Inputs may be any that keep to these rules, and one draw needn't show every extreme that they name: window_start[t] = max(first position of token t's document, t - 1023); documents are runs of consecutive tokens, the last token begins a document of its own, and t - window_start[t] equals 1023 for some token.
All inputs are finite; a program needn't handle non-finite values.
Results may differ from the reference program's by a relative error of at most 0.014.
Values may be sent and summed in bfloat16 or wider, within the bound.
A program may use at most 128 MiB of HBM per device.

```python
import jax
import jax.numpy as jnp
from jax import lax

QUERY_HEAD_COUNT = 32
KEY_VALUE_HEADS = 16
HEAD_SIZE = 128
WINDOW_LENGTH = 1024
SHARD_TOKENS = 256
SLAB_TOKENS = 4096
N_SEQ = 16


grad_level = 16.0


def draw_window_start(key, part):
    position = jnp.arange(SLAB_TOKENS, dtype=jnp.int32)
    marker = jax.random.randint(jax.random.fold_in(key, 11), (SLAB_TOKENS,), 0, 3 * WINDOW_LENGTH)
    begins = (marker == 0) & (position > WINDOW_LENGTH) | (position == 0) | (position == SLAB_TOKENS - 1)
    doc_first = lax.cummax(jnp.where(begins, position, 0), axis=0)
    return jnp.maximum(doc_first, position - WINDOW_LENGTH + 1).astype(jnp.int32)


def draw_output_gradient(key, part):
    full_shape = (SLAB_TOKENS, QUERY_HEAD_COUNT, HEAD_SIZE)
    sample_key = jax.random.fold_in(key, 23)
    fraction = jnp.arange(SLAB_TOKENS, dtype=jnp.float32) / SLAB_TOKENS
    sample = jnp.clip(jax.random.normal(sample_key, full_shape, jnp.float32), -6.0, 6.0)
    scale_ramp = 1.0 + 2.0 * fraction
    return (grad_level * sample * scale_ramp[:, None, None]).astype(jnp.bfloat16)


def block_levels(stream_key, extent, shards, low, top_value):
    loudness, own = 1.0, jax.random.fold_in(stream_key, 6)
    for axis_at, blocks in shards:
        steps = jnp.exp(jax.random.uniform(jax.random.fold_in(own, axis_at), (blocks,), jnp.float32, low / len(shards), top_value / len(shards)))
        loudness = loudness * jnp.repeat(steps, extent[axis_at] // blocks).reshape([-1 if axis == axis_at else 1 for axis in range(len(extent))])
    return loudness


def centred(stream_key, shape, spread, reach, pieces=(), kind=jnp.bfloat16):
    level = block_levels(stream_key, shape, pieces, -0.22, 0.18) if pieces else 1.0
    drawn = jax.random.normal(stream_key, shape, jnp.float32) * spread * level
    return jnp.minimum(jnp.maximum(drawn, -reach), reach).astype(kind)


def setup_inputs(seed: int = 0) -> dict:
    arg_keys = jax.random.split(jax.random.key(seed), 8)
    return {
        "queries": centred(arg_keys[0], (SLAB_TOKENS, QUERY_HEAD_COUNT, HEAD_SIZE), 1.0, 6.0, ((0, 16), (1, 2))),
        "keys": centred(arg_keys[1], (SLAB_TOKENS, KEY_VALUE_HEADS, HEAD_SIZE), 1.0, 6.0, ((0, 16), (1, 2))),
        "values": centred(arg_keys[2], (SLAB_TOKENS, KEY_VALUE_HEADS, HEAD_SIZE), 1.0, 6.0, ((0, 16), (1, 2))),
        "output_gradient": draw_output_gradient(jax.random.fold_in(arg_keys[7], 71), 0),
        "window_start": draw_window_start(jax.random.fold_in(arg_keys[7], 71), 0),
        "query_gain": jnp.clip(1.0 + 0.18 * jax.random.normal(arg_keys[5], (HEAD_SIZE,), jnp.float32), 0.1, 1.9),
        "key_gain": jnp.clip(1.0 + 0.18 * jax.random.normal(arg_keys[6], (HEAD_SIZE,), jnp.float32), 0.1, 1.9),
    }


attn_scale = 168.0 ** (-0.5)
norm_eps = 1e-06
rope_base = 10000.0

def rotary_tables(positions, head_width):
    half_width = head_width // 2
    frequency = rope_base ** (-(jnp.arange(half_width, dtype=jnp.float32) * 2.0) / head_width)
    angles = positions.astype(jnp.float32)[:, None] * frequency[None, :]
    return (jnp.cos(angles)[:, None, :], jnp.sin(angles)[:, None, :])

def rotate(tensor, cos_table, sin_table):
    half_width = tensor.shape[-1] // 2
    first_half = tensor[..., :half_width]
    second_half = tensor[..., half_width:]
    return jnp.concatenate([first_half * cos_table - second_half * sin_table, second_half * cos_table + first_half * sin_table], axis=-1)

def unrotate(tensor, cos_table, sin_table):
    half_width = tensor.shape[-1] // 2
    first_half = tensor[..., :half_width]
    second_half = tensor[..., half_width:]
    return jnp.concatenate([first_half * cos_table + second_half * sin_table, second_half * cos_table - first_half * sin_table], axis=-1)

def normalize(tensor, gain_vec):
    tensor = tensor.astype(jnp.float32)
    inv_rms = lax.rsqrt(lax.optimization_barrier(jnp.mean(tensor * tensor, axis=-1, keepdims=True)) + norm_eps)
    unit_tensor = tensor * inv_rms
    return (unit_tensor, inv_rms, unit_tensor * gain_vec)

def norm_back(grad_norm, unit_tensor, inv_rms, gain_vec):
    grad_unit = grad_norm * gain_vec
    grad_tensor = inv_rms * (grad_unit - unit_tensor * lax.optimization_barrier(jnp.mean(grad_unit * unit_tensor, axis=-1, keepdims=True)))
    grad_gain = lax.optimization_barrier(jnp.sum(grad_norm * unit_tensor, axis=(0, 1)))
    return (grad_tensor, grad_gain)

def rounded(tensor):
    return lax.optimization_barrier(tensor.astype(jnp.bfloat16)).astype(jnp.float32)

def reference(queries, keys, values, output_gradient, window_start, query_gain, key_gain):
    positions = jnp.arange(SLAB_TOKENS, dtype=jnp.int32)
    cos_table, sin_table = rotary_tables(positions, HEAD_SIZE)
    query_unit, query_inv, query_normed = normalize(queries, query_gain)
    key_unit, key_inv, key_normed = normalize(keys, key_gain)
    rotated_query = rotate(query_normed, cos_table, sin_table).astype(jnp.bfloat16)
    rotated_key = rotate(key_normed, cos_table, sin_table).astype(jnp.bfloat16)
    group_count = QUERY_HEAD_COUNT // KEY_VALUE_HEADS
    reach_count = WINDOW_LENGTH // SHARD_TOKENS
    keys_padded_front = jnp.concatenate([jnp.zeros((WINDOW_LENGTH, KEY_VALUE_HEADS, HEAD_SIZE), jnp.bfloat16), rotated_key], axis=0)
    values_padded_front = jnp.concatenate([jnp.zeros((WINDOW_LENGTH, KEY_VALUE_HEADS, HEAD_SIZE), jnp.bfloat16), values], axis=0)
    span_rows = WINDOW_LENGTH + SHARD_TOKENS

    def block_step(carried, block_idx):
        key_sums, value_sums = carried
        first_row_index = (block_idx * SHARD_TOKENS).astype(jnp.int32)
        block_queries = lax.dynamic_slice_in_dim(rotated_query, first_row_index, SHARD_TOKENS, 0).reshape(SHARD_TOKENS, KEY_VALUE_HEADS, group_count, HEAD_SIZE).astype(jnp.float32)
        block_gradient = lax.dynamic_slice_in_dim(output_gradient, first_row_index, SHARD_TOKENS, 0).reshape(SHARD_TOKENS, KEY_VALUE_HEADS, group_count, HEAD_SIZE).astype(jnp.float32)
        key_block = lax.dynamic_slice_in_dim(keys_padded_front, first_row_index, span_rows, 0).astype(jnp.float32)
        value_block = lax.dynamic_slice_in_dim(values_padded_front, first_row_index, span_rows, 0).astype(jnp.float32)
        start_block = lax.dynamic_slice_in_dim(window_start, first_row_index, SHARD_TOKENS, 0)
        query_pos = first_row_index + jnp.arange(SHARD_TOKENS, dtype=jnp.int32)
        key_pos = first_row_index - WINDOW_LENGTH + jnp.arange(span_rows, dtype=jnp.int32)
        visible = (key_pos[None, :] >= start_block[:, None]) & (key_pos[None, :] <= query_pos[:, None])
        scores = attn_scale * jnp.einsum('tgrd,kgd->grtk', block_queries, key_block)
        exp_scores = jnp.where(visible, jnp.exp(scores), 0.0)
        row_total = lax.optimization_barrier(jnp.sum(exp_scores, axis=-1, keepdims=True))
        weights = exp_scores / row_total
        weights_b = weights.astype(jnp.bfloat16)
        weights_b = lax.optimization_barrier(weights_b).astype(jnp.float32)
        attended = jnp.einsum('grtk,kgd->grtd', weights_b, value_block)
        row_delta = lax.optimization_barrier(jnp.sum(jnp.transpose(block_gradient, (1, 2, 0, 3)) * attended, axis=-1))
        grad_weights = jnp.einsum('tgrd,kgd->grtk', block_gradient, value_block)
        grad_scores = (weights * (grad_weights - row_delta[..., None]) * attn_scale).astype(jnp.bfloat16)
        grad_scores = lax.optimization_barrier(grad_scores).astype(jnp.float32)
        query_part = jnp.einsum('grtk,kgd->tgrd', grad_scores, key_block)
        key_part = jnp.einsum('grtk,tgrd->kgd', grad_scores, block_queries)
        value_part = jnp.einsum('grtk,tgrd->kgd', weights_b, block_gradient)
        for index in range(reach_count + 1):
            target = (first_row_index + index * SHARD_TOKENS).astype(jnp.int32)
            key_piece = key_part[index * SHARD_TOKENS:(index + 1) * SHARD_TOKENS]
            value_piece = value_part[index * SHARD_TOKENS:(index + 1) * SHARD_TOKENS]
            key_now = lax.dynamic_slice_in_dim(key_sums, target, SHARD_TOKENS, 0)
            value_now = lax.dynamic_slice_in_dim(value_sums, target, SHARD_TOKENS, 0)
            if index < reach_count:
                key_new = rounded(key_now + rounded(key_piece))
                value_new = rounded(value_now + rounded(value_piece))
            else:
                key_new = key_now + key_piece
                value_new = value_now + value_piece
            key_sums = lax.dynamic_update_slice_in_dim(key_sums, key_new, target, 0)
            value_sums = lax.dynamic_update_slice_in_dim(value_sums, value_new, target, 0)
        return ((key_sums, value_sums), query_part.reshape(SHARD_TOKENS, QUERY_HEAD_COUNT, HEAD_SIZE))
    blank_rows = jnp.zeros((WINDOW_LENGTH + SLAB_TOKENS, KEY_VALUE_HEADS, HEAD_SIZE), jnp.float32)
    (key_sums, value_sums), query_parts = lax.scan(block_step, (blank_rows, blank_rows), jnp.arange(N_SEQ, dtype=jnp.int32), reverse=True)
    query_rot_grad = query_parts.reshape(SLAB_TOKENS, QUERY_HEAD_COUNT, HEAD_SIZE)
    query_normed_grad = unrotate(query_rot_grad, cos_table, sin_table)
    query_grad, query_gain_grad = norm_back(query_normed_grad, query_unit, query_inv, query_gain)
    key_normed_grad = unrotate(key_sums[WINDOW_LENGTH:], cos_table, sin_table)
    key_grad, key_gain_grad = norm_back(key_normed_grad, key_unit, key_inv, key_gain)
    value_grad = value_sums[WINDOW_LENGTH:].astype(jnp.bfloat16)
    return (query_grad.astype(jnp.bfloat16), key_grad.astype(jnp.bfloat16), value_grad, query_gain_grad, key_gain_grad)
```

```python
import functools
import math

import jax
import jax.numpy as jnp
from jax import lax
from jax.experimental import pallas as pl
from jax.experimental.pallas import tpu as pltpu
from jax.sharding import PartitionSpec as P

WINDOW_LENGTH = 1024

attn_scale = 168.0 ** (-0.5)
norm_eps = 1e-06
rope_base = 10000.0
log2_e = math.log2(math.e)
f32 = jnp.float32
bf16 = jnp.bfloat16


def hop(value, axis, step):
    count = lax.axis_size(axis)
    initial, last = (max(0, -step), min(count, count - step))
    return lax.ppermute(value, axis, [(source, source + step) for source in range(initial, last)])


def rotary_tables(positions, head_width):
    half_width = head_width // 2
    frequency = rope_base ** (-(jnp.arange(half_width, dtype=f32) * 2.0) / head_width)
    angles = positions.astype(f32)[:, None] * frequency[None, :]
    cos, sin = jnp.cos(angles), jnp.sin(angles)
    return (jnp.concatenate([cos, cos], axis=-1), jnp.concatenate([-sin, sin], axis=-1))


def swap_halves(x):
    half = x.shape[-1] // 2
    return jnp.concatenate([x[:, half:], x[:, :half]], axis=-1)


def normalize(x, gain):
    x = x.astype(f32)
    inv = lax.rsqrt(jnp.mean(x * x, axis=-1, keepdims=True) + norm_eps)
    unit = x * inv
    return unit, inv, unit * gain


def norm_back(rot_grad, unit, inv, gain, cos, sin):
    grad = rot_grad * cos - swap_halves(rot_grad) * sin
    grad_unit = grad * gain
    out = inv * (grad_unit - unit * jnp.mean(grad_unit * unit, axis=-1, keepdims=True))
    part = grad * unit
    return out, jnp.sum(part.reshape(part.shape[0] // 8, 8, part.shape[1]), axis=0)


def dot(a, b, ca, cb):
    return lax.dot_general(a, b, (((ca,), (cb,)), ((), ())), preferred_element_type=f32)


def prep_kernel(k_ref, v_ref, gain_ref, cos_ref, sin_ref, kv_ref):
    heads, _, rows, width = kv_ref.shape
    for g in range(heads):
        cols = slice(g * width, (g + 1) * width)
        _, _, normed = normalize(k_ref[:, cols], gain_ref[...])
        rot = normed * cos_ref[...] + swap_halves(normed) * sin_ref[...]
        kv_ref[g, 0] = rot.astype(bf16)
        kv_ref[g, 1] = v_ref[:, cols]


def attn_kernel(blocks, group, *refs):
    q_ref, do_ref, low_ref, gain_ref, cos_ref, sin_ref = refs[:6]
    kv = refs[6 : 6 + blocks]
    dq_ref, part_ref = refs[6 + blocks : 8 + blocks]
    terms = refs[8 + blocks : 8 + 2 * blocks]
    e_scr, gw_scr = refs[8 + 2 * blocks :]
    rows, width = cos_ref.shape
    cos, sin, gain = cos_ref[...], sin_ref[...], gain_ref[...]
    rots, saved = [], []
    for h in range(group):
        unit, inv, normed = normalize(q_ref[:, h * width : (h + 1) * width], gain)
        rots.append((normed * cos + swap_halves(normed) * sin).astype(bf16))
    q = jnp.concatenate(rots, axis=0)
    do = jnp.concatenate([do_ref[:, h * width : (h + 1) * width] for h in range(group)], axis=0)
    low = low_ref[...]
    shape = (rows, rows * group)
    key_iota = lax.broadcasted_iota(jnp.int32, shape, 0)
    query_iota = lax.rem(lax.broadcasted_iota(jnp.int32, (1, rows * group), 1), rows)
    total = jnp.zeros((1, rows * group), f32)
    for j in range(blocks):
        s = dot(kv[j][0, 0], q, 1, 1)
        e = jnp.exp2(s * (attn_scale * log2_e))
        seen = key_iota >= low - j * rows
        if j == blocks - 1:
            seen = seen & (key_iota <= query_iota)
        e = jnp.where(seen, e, 0.0)
        total = total + jnp.sum(e, axis=0, keepdims=True)
        e_scr[j] = e
    inv_total = 1.0 / total
    delta = jnp.zeros((1, rows * group), f32)
    for j in range(blocks):
        w = e_scr[j] * inv_total
        wb = w.astype(bf16)
        gw = dot(kv[j][0, 1], do, 1, 1)
        delta = delta + jnp.sum(wb.astype(f32) * gw, axis=0, keepdims=True)
        gw_scr[j] = gw
        e_scr[j] = w
        terms[j][0, 1] = dot(wb, do, 1, 0).astype(terms[j].dtype)
    dq_t = jnp.zeros((width, rows * group), f32)
    for j in range(blocks):
        gs = (e_scr[j] * (gw_scr[j] - delta) * attn_scale).astype(bf16)
        dq_t = dq_t + dot(kv[j][0, 0], gs, 0, 0)
        terms[j][0, 0] = dot(gs, q, 1, 0).astype(terms[j].dtype)
    dq = dq_t.T
    part = jnp.zeros((8, width), f32)
    for h in range(group):
        unit, inv, _ = normalize(q_ref[:, h * width : (h + 1) * width], gain)
        out, p = norm_back(dq[h * rows : (h + 1) * rows], unit, inv, gain, cos, sin)
        dq_ref[:, h * width : (h + 1) * width] = out.astype(bf16)
        part = part + p
    part_ref[0] = part


def final_kernel(carry_ref, term_ref, k_ref, gain_ref, cos_ref, sin_ref, dk_ref, dv_ref, part_ref):
    heads, _, rows, width = term_ref.shape
    gain, cos, sin = gain_ref[...], cos_ref[...], sin_ref[...]
    part = jnp.zeros((8, width), f32)
    for g in range(heads):
        cols = slice(g * width, (g + 1) * width)
        unit, inv, _ = normalize(k_ref[:, cols], gain)
        dk = carry_ref[g, 0].astype(f32) + term_ref[g, 0]
        out, p = norm_back(dk, unit, inv, gain, cos, sin)
        dk_ref[:, cols] = out.astype(bf16)
        dv_ref[:, cols] = (carry_ref[g, 1].astype(f32) + term_ref[g, 1]).astype(bf16)
        part = part + p
    part_ref[...] = part


def body(queries, keys, values, output_gradient, window_start, query_gain, key_gain):
    rows, q_heads, width = queries.shape
    kv_heads = keys.shape[1]
    group = q_heads // kv_heads
    reach = WINDOW_LENGTH // rows
    blocks = reach + 1
    first = lax.axis_index("seq") * rows
    cos, sin = rotary_tables(first + jnp.arange(rows, dtype=jnp.int32), width)
    low = jnp.tile(window_start - first + reach * rows, group)[None, :]
    q2 = queries.reshape(rows, q_heads * width)
    do2 = output_gradient.reshape(rows, q_heads * width)
    k2 = keys.reshape(rows, kv_heads * width)
    v2 = values.reshape(rows, kv_heads * width)
    q_gain, k_gain = query_gain[None, :], key_gain[None, :]
    params = pltpu.CompilerParams(vmem_limit_bytes=56 * 1024 * 1024)
    kv_shape = (kv_heads, 2, rows, width)
    kv = pl.pallas_call(
        prep_kernel, out_shape=jax.ShapeDtypeStruct(kv_shape, bf16), compiler_params=params
    )(k2, v2, k_gain, cos, sin)
    held = [kv]
    for _ in range(reach):
        held.append(hop(held[-1], "seq", 1))
    held = held[::-1]

    whole = lambda a: pl.BlockSpec(a.shape, lambda g: (0,) * a.ndim)
    head = pl.BlockSpec((1, 2, rows, width), lambda g: (g, 0, 0, 0))
    pair = pl.BlockSpec((rows, group * width), lambda g: (0, g))
    outs = pl.pallas_call(
        functools.partial(attn_kernel, blocks, group),
        grid=(kv_heads,),
        in_specs=[pair, pair, whole(low), whole(q_gain), whole(cos), whole(sin)] + [head] * blocks,
        out_specs=[pair, pl.BlockSpec((1, 8, width), lambda g: (g, 0, 0))] + [head] * blocks,
        out_shape=[
            jax.ShapeDtypeStruct(q2.shape, bf16),
            jax.ShapeDtypeStruct((kv_heads, 8, width), f32),
        ]
        + [jax.ShapeDtypeStruct(kv_shape, bf16)] * reach
        + [jax.ShapeDtypeStruct(kv_shape, f32)],
        scratch_shapes=[pltpu.VMEM((blocks, rows, rows * group), f32)] * 2,
        compiler_params=params,
    )(q2, do2, low, q_gain, cos, sin, *held)
    dq, q_part = outs[:2]
    terms = outs[2:]
    carry = terms[0]
    for k in range(reach):
        carry = hop(carry, "seq", -1)
        if k < reach - 1:
            carry = (carry.astype(f32) + terms[k + 1].astype(f32)).astype(bf16)
    dk, dv, k_part = pl.pallas_call(
        final_kernel,
        out_shape=[
            jax.ShapeDtypeStruct(k2.shape, bf16),
            jax.ShapeDtypeStruct(k2.shape, bf16),
            jax.ShapeDtypeStruct((8, width), f32),
        ],
        compiler_params=params,
    )(carry, terms[-1], k2, k_gain, cos, sin)
    parts = jnp.stack([jnp.sum(q_part, axis=(0, 1)), jnp.sum(k_part, axis=0)])
    gains = lax.psum(parts, ("seq", "kv"))
    return (
        dq.reshape(queries.shape),
        dk.reshape(keys.shape),
        dv.reshape(values.shape),
        gains[0],
        gains[1],
    )


def solution(mesh):
    split = P("seq", "kv", None)
    return jax.shard_map(
        body,
        mesh=mesh,
        in_specs=(split, split, split, split, P("seq"), P(), P()),
        out_specs=(split, split, split, P(), P()),
        check_vma=False,
    )
```

```python
import functools
import math

import jax
import jax.numpy as jnp
from jax import lax
from jax.experimental import pallas as pl
from jax.experimental.pallas import tpu as pltpu
from jax.sharding import PartitionSpec as P

WINDOW_LENGTH = 1024

attn_scale = 168.0 ** (-0.5)
norm_eps = 1e-06
rope_base = 10000.0
log2_e = math.log2(math.e)
f32 = jnp.float32
bf16 = jnp.bfloat16


def rotary_tables(positions, head_width):
    half_width = head_width // 2
    frequency = rope_base ** (-(jnp.arange(half_width, dtype=f32) * 2.0) / head_width)
    angles = positions.astype(f32)[:, None] * frequency[None, :]
    cos, sin = jnp.cos(angles), jnp.sin(angles)
    return (jnp.concatenate([cos, cos], axis=-1), jnp.concatenate([-sin, sin], axis=-1))


def swap_halves(x):
    half = x.shape[-1] // 2
    return jnp.concatenate([x[:, half:], x[:, :half]], axis=-1)


def normalize(x, gain):
    x = x.astype(f32)
    inv = lax.rsqrt(jnp.mean(x * x, axis=-1, keepdims=True) + norm_eps)
    unit = x * inv
    return unit, inv, unit * gain


def norm_back(rot_grad, unit, inv, gain, cos, sin):
    grad = rot_grad * cos - swap_halves(rot_grad) * sin
    grad_unit = grad * gain
    out = inv * (grad_unit - unit * jnp.mean(grad_unit * unit, axis=-1, keepdims=True))
    part = grad * unit
    return out, jnp.sum(part.reshape(part.shape[0] // 8, 8, part.shape[1]), axis=0)


def dot(a, b, ca, cb):
    return lax.dot_general(a, b, (((ca,), (cb,)), ((), ())), preferred_element_type=f32)


def fused_kernel(
    n_seq, n_kv, reach, group,
    q_ref, do_ref, k_ref, v_ref, low_ref, qg_ref, kg_ref, cos_ref, sin_ref,
    dq_ref, dk_ref, dv_ref, gains_ref,
    kvbuf, tbuf, rbuf, own, e_scr, gw_scr, part_scr, gbuf, gstage,
    kv_send, kv_recv, t_send, t_recv, g_send, g_recv,
):
    blocks = reach + 1
    lag = 3
    heads, rows, width = kvbuf.shape[1], kvbuf.shape[3], kvbuf.shape[4]
    wide = rows * group
    d = lax.axis_index("seq")
    x = lax.axis_index("kv")
    mesh_ids = pl.DeviceIdType.MESH

    partners = []
    step = 1
    while step < n_seq:
        up = lax.rem(lax.div(d, step), 2)
        partners.append((d + step - 2 * step * up, x))
        step *= 2
    step = 1
    while step < n_kv:
        up = lax.rem(lax.div(x, step), 2)
        partners.append((d, x + step - 2 * step * up))
        step *= 2

    barrier = pltpu.get_barrier_semaphore()
    for p in partners:
        pl.semaphore_signal(barrier, inc=1, device_id=p, device_id_type=mesh_ids)

    @pl.when(d > 0)
    def _():
        pl.semaphore_signal(barrier, inc=1, device_id=(d - 1, x), device_id_type=mesh_ids)

    @pl.when(d < n_seq - 1)
    def _():
        pl.semaphore_signal(barrier, inc=1, device_id=(d + 1, x), device_id_type=mesh_ids)

    @pl.when(d >= 4)
    def _():
        pl.semaphore_signal(barrier, inc=1, device_id=(d - 4, x), device_id_type=mesh_ids)

    @pl.when(d < n_seq - 4)
    def _():
        pl.semaphore_signal(barrier, inc=1, device_id=(d + 4, x), device_id_type=mesh_ids)

    def some(count):
        return lax.div(count + n_seq - 1, n_seq)

    after = n_seq - 1 - d
    peers = some(d) + some(after) + some(lax.div(d, 4)) + some(lax.div(after, 4))
    pl.semaphore_wait(barrier, len(partners) + peers)

    core = lax.rem(d, 2)
    high = lax.rem(lax.div(d, 2), 2)
    mate = d + 1 - 2 * core
    routes = [
        (0, 4, d + 4, d < n_seq - 4),
        (0, 2, d + 2, high == 0),
        (0, 1, d + 1, core == 0),
        (4, 3, d - 1, (core == 1) & (d >= 4)),
        (4, 2, d - 2, (high == 1) & (d >= 4)),
        (2, 3, d + 1, (core == 0) & (d >= 2)),
        (2, 1, d - 1, (core == 1) & (d >= 2)),
    ]

    def kv_copy(r, g):
        source, target, where, _ = routes[r]
        return pltpu.make_async_remote_copy(
            src_ref=kvbuf.at[source, g], dst_ref=kvbuf.at[target, g],
            send_sem=kv_send.at[r, g], recv_sem=kv_recv.at[target - 1, g],
            device_id=(where, x), device_id_type=mesh_ids,
        )

    def kv_start(r, g):
        @pl.when(routes[r][3])
        def _():
            kv_copy(r, g).start()

    def kv_wait(slot, g):
        pltpu.make_async_remote_copy(
            src_ref=kvbuf.at[0, g], dst_ref=kvbuf.at[slot, g],
            send_sem=kv_send.at[0, g], recv_sem=kv_recv.at[slot - 1, g],
            device_id=(mate, x), device_id_type=mesh_ids,
        ).wait_recv()

    def term_copy(i, g):
        return pltpu.make_async_remote_copy(
            src_ref=tbuf.at[i, g], dst_ref=rbuf.at[i, g],
            send_sem=t_send.at[i, g], recv_sem=t_recv.at[i, g],
            device_id=(d - 1, x), device_id_type=mesh_ids,
        )

    def term_sends(i):
        return d >= reach - i

    def term_arrives(i):
        return (d >= reach - i - 1) & (d < n_seq - 1)

    for k in range(1, blocks):
        @pl.when(d < k)
        def _():
            kvbuf[k] = jnp.zeros(kvbuf.shape[1:], bf16)

    @pl.when(d == n_seq - 1)
    def _():
        rbuf[reach - 1] = jnp.zeros(rbuf.shape[1:], bf16)

    part_scr[...] = jnp.zeros(part_scr.shape, f32)

    def prep(g):
        cols = pl.ds(pl.multiple_of(g * width, width), width)
        _, _, normed = normalize(k_ref[:, cols], kg_ref[...])
        rot = normed * cos_ref[...] + swap_halves(normed) * sin_ref[...]
        kvbuf[0, g, 0] = rot.astype(bf16)
        kvbuf[0, g, 1] = v_ref[:, cols]

    def attend(g):
        cos, sin, gain = cos_ref[...], sin_ref[...], qg_ref[...]
        cols = [
            pl.ds(pl.multiple_of((g * group + h) * width, width), width) for h in range(group)
        ]
        rots = []
        for h in range(group):
            _, _, normed = normalize(q_ref[:, cols[h]], gain)
            rots.append((normed * cos + swap_halves(normed) * sin).astype(bf16))
        q = jnp.concatenate(rots, axis=0)
        do = jnp.concatenate([do_ref[:, c] for c in cols], axis=0)
        low = low_ref[...]
        key_iota = lax.broadcasted_iota(jnp.int32, (rows, wide), 0)
        query_iota = lax.rem(lax.broadcasted_iota(jnp.int32, (1, wide), 1), rows)
        total = jnp.zeros((1, wide), f32)
        for j in range(blocks):
            s = dot(kvbuf[reach - j, g, 0], q, 1, 1)
            e = jnp.exp2(s * (attn_scale * log2_e))
            seen = key_iota >= low - j * rows
            if j == blocks - 1:
                seen = seen & (key_iota <= query_iota)
            e = jnp.where(seen, e, 0.0)
            total = total + jnp.sum(e, axis=0, keepdims=True)
            e_scr[j] = e
        inv_total = 1.0 / total
        delta = jnp.zeros((1, wide), f32)
        for j in range(blocks):
            w = e_scr[j] * inv_total
            wb = w.astype(bf16)
            gw = dot(kvbuf[reach - j, g, 1], do, 1, 1)
            delta = delta + jnp.sum(wb.astype(f32) * gw, axis=0, keepdims=True)
            gw_scr[j] = gw
            e_scr[j] = w
            term = dot(wb, do, 1, 0)
            if j < reach:
                tbuf[j, g, 1] = term.astype(bf16)
            else:
                own[g, 1] = term
        dq_t = jnp.zeros((width, wide), f32)
        for j in range(blocks):
            gs = (e_scr[j] * (gw_scr[j] - delta) * attn_scale).astype(bf16)
            dq_t = dq_t + dot(kvbuf[reach - j, g, 0], gs, 0, 0)
            term = dot(gs, q, 1, 0)
            if j < reach:
                tbuf[j, g, 0] = term.astype(bf16)
            else:
                own[g, 0] = term
        dq = dq_t.T
        for h in range(group):
            unit, inv, _ = normalize(q_ref[:, cols[h]], gain)
            out, p = norm_back(dq[h * rows : (h + 1) * rows], unit, inv, gain, cos, sin)
            dq_ref[:, cols[h]] = out.astype(bf16)
            part_scr[0] += p

    def finish(g):
        cols = pl.ds(pl.multiple_of(g * width, width), width)
        gain = kg_ref[...]
        unit, inv, _ = normalize(k_ref[:, cols], gain)
        dk = rbuf[reach - 1, g, 0].astype(f32) + own[g, 0]
        out, p = norm_back(dk, unit, inv, gain, cos_ref[...], sin_ref[...])
        dk_ref[:, cols] = out.astype(bf16)
        dv_ref[:, cols] = (rbuf[reach - 1, g, 1].astype(f32) + own[g, 1]).astype(bf16)
        part_scr[1] += p

    def turn(t, _):
        @pl.when(t < heads)
        def _():
            prep(t)

            for r in range(3):
                kv_start(r, t)

        g1 = t - 1

        @pl.when((g1 >= 0) & (g1 < heads))
        def _():
            @pl.when(d >= 4)
            def _():
                kv_wait(4, g1)
                kv_start(3, g1)
                kv_start(4, g1)

            @pl.when(high == 1)
            def _():
                kv_wait(2, g1)
                kv_start(5, g1)
                kv_start(6, g1)

        g2 = t - 2

        @pl.when((g2 >= 0) & (g2 < heads) & (high == 0) & (d >= 4))
        def _():
            kv_wait(2, g2)
            kv_start(5, g2)
            kv_start(6, g2)

        for i in range(1, reach):
            g = t - lag - i

            @pl.when((g >= 0) & (g < heads) & term_sends(i))
            def _():
                @pl.when(d < n_seq - 1)
                def _():
                    term_copy(i - 1, g).wait_recv()
                    tbuf[i, g] = (tbuf[i, g].astype(f32) + rbuf[i - 1, g].astype(f32)).astype(bf16)

                term_copy(i, g).start()

        g = t - lag

        @pl.when((g >= 0) & (g < heads))
        def _():
            @pl.when(d >= 1)
            def _():
                kv_wait(1, g)

            @pl.when(d >= 3)
            def _():
                kv_wait(3, g)

            attend(g)

            @pl.when(term_sends(0))
            def _():
                term_copy(0, g).start()

        f = t - lag - reach

        @pl.when((f >= 0) & (f < heads))
        def _():
            @pl.when(d < n_seq - 1)
            def _():
                term_copy(reach - 1, f).wait_recv()

            finish(f)

        return 0

    lax.fori_loop(0, heads + lag + reach, turn, 0)

    q_part = jnp.sum(part_scr[0], axis=0, keepdims=True)
    k_part = jnp.sum(part_scr[1], axis=0, keepdims=True)
    row = lax.broadcasted_iota(jnp.int32, (8, width), 0)
    total = jnp.where(row == 0, q_part, jnp.where(row == 1, k_part, 0.0))
    for r, p in enumerate(partners):
        gstage[r] = total
        copy = pltpu.make_async_remote_copy(
            src_ref=gstage.at[r], dst_ref=gbuf.at[r],
            send_sem=g_send.at[r], recv_sem=g_recv.at[r],
            device_id=p, device_id_type=mesh_ids,
        )
        copy.start()
        copy.wait()
        total = total + gbuf[r]
    gains_ref[...] = total

    def drain(g, _):
        for k in range(reach):
            @pl.when(term_sends(k))
            def _():
                term_copy(k, g).wait_send()

        for r in range(len(routes)):
            @pl.when(routes[r][3])
            def _():
                kv_copy(r, g).wait_send()

        return 0

    lax.fori_loop(0, heads, drain, 0)


def body(n_seq, n_kv, queries, keys, values, output_gradient, window_start, query_gain, key_gain):
    rows, q_heads, width = queries.shape
    kv_heads = keys.shape[1]
    group = q_heads // kv_heads
    reach = WINDOW_LENGTH // rows
    blocks = reach + 1
    first = lax.axis_index("seq") * rows
    cos, sin = rotary_tables(first + jnp.arange(rows, dtype=jnp.int32), width)
    low = jnp.tile(window_start - first + reach * rows, group)[None, :]
    q2 = queries.reshape(rows, q_heads * width)
    do2 = output_gradient.reshape(rows, q_heads * width)
    k2 = keys.reshape(rows, kv_heads * width)
    v2 = values.reshape(rows, kv_heads * width)
    rounds = (n_seq - 1).bit_length() + (n_kv - 1).bit_length()
    chunk = (kv_heads, 2, rows, width)
    dma = pltpu.SemaphoreType.DMA
    dq, dk, dv, gains = pl.pallas_call(
        functools.partial(fused_kernel, n_seq, n_kv, reach, group),
        out_shape=[
            jax.ShapeDtypeStruct(q2.shape, bf16),
            jax.ShapeDtypeStruct(k2.shape, bf16),
            jax.ShapeDtypeStruct(k2.shape, bf16),
            jax.ShapeDtypeStruct((8, width), f32),
        ],
        in_specs=[pl.BlockSpec(memory_space=pltpu.VMEM)] * 9,
        out_specs=[pl.BlockSpec(memory_space=pltpu.VMEM)] * 4,
        scratch_shapes=[
            pltpu.VMEM((blocks,) + chunk, bf16),
            pltpu.VMEM((reach,) + chunk, bf16),
            pltpu.VMEM((reach,) + chunk, bf16),
            pltpu.VMEM(chunk, f32),
            pltpu.VMEM((blocks, rows, rows * group), f32),
            pltpu.VMEM((blocks, rows, rows * group), f32),
            pltpu.VMEM((2, 8, width), f32),
            pltpu.VMEM((rounds, 8, width), f32),
            pltpu.VMEM((rounds, 8, width), f32),
        ]
        + [dma((7, kv_heads))]
        + [dma((reach, kv_heads))] * 3
        + [dma((rounds,))] * 2,
        compiler_params=pltpu.CompilerParams(
            collective_id=0, has_side_effects=True, vmem_limit_bytes=50 * 1024 * 1024
        ),
    )(q2, do2, k2, v2, low, query_gain[None, :], key_gain[None, :], cos, sin)
    return (
        dq.reshape(queries.shape),
        dk.reshape(keys.shape),
        dv.reshape(values.shape),
        gains[0],
        gains[1],
    )


def solution(mesh):
    split = P("seq", "kv", None)
    return jax.shard_map(
        functools.partial(body, mesh.shape["seq"], mesh.shape["kv"]),
        mesh=mesh,
        in_specs=(split, split, split, split, P("seq"), P(), P()),
        out_specs=(split, split, split, P(), P()),
        check_vma=False,
    )
```

```python
import functools
import math

import jax
import jax.numpy as jnp
from jax import lax
from jax.experimental import pallas as pl
from jax.experimental.pallas import tpu as pltpu
from jax.sharding import PartitionSpec as P

WINDOW_LENGTH = 1024

attn_scale = 168.0 ** (-0.5)
norm_eps = 1e-06
rope_base = 10000.0
log2_e = math.log2(math.e)
f32 = jnp.float32
bf16 = jnp.bfloat16


def rotary_tables(positions, head_width):
    half_width = head_width // 2
    frequency = rope_base ** (-(jnp.arange(half_width, dtype=f32) * 2.0) / head_width)
    angles = positions.astype(f32)[:, None] * frequency[None, :]
    cos, sin = jnp.cos(angles), jnp.sin(angles)
    return (jnp.concatenate([cos, cos], axis=-1), jnp.concatenate([-sin, sin], axis=-1))


def swap_halves(x):
    half = x.shape[-1] // 2
    return jnp.concatenate([x[:, half:], x[:, :half]], axis=-1)


def normalize(x, gain):
    x = x.astype(f32)
    inv = lax.rsqrt(jnp.mean(x * x, axis=-1, keepdims=True) + norm_eps)
    unit = x * inv
    return unit, inv, unit * gain


def norm_back(rot_grad, unit, inv, gain, cos, sin):
    grad = rot_grad * cos - swap_halves(rot_grad) * sin
    grad_unit = grad * gain
    out = inv * (grad_unit - unit * jnp.mean(grad_unit * unit, axis=-1, keepdims=True))
    part = grad * unit
    return out, jnp.sum(part.reshape(part.shape[0] // 8, 8, part.shape[1]), axis=0)


def dot(a, b, ca, cb):
    return lax.dot_general(a, b, (((ca,), (cb,)), ((), ())), preferred_element_type=f32)


def fused_kernel(
    n_seq, n_kv, reach, group,
    q_ref, do_ref, k_ref, v_ref, low_ref, qg_ref, kg_ref, cos_ref, sin_ref,
    dq_ref, dk_ref, dv_ref, gains_ref,
    kvbuf, tbuf, rbuf, own, e_scr, gw_scr, part_scr, gbuf, gstage,
    kv_send, kv_recv, t_send, t_recv, g_send, g_recv,
):
    blocks = reach + 1
    lag = 3
    heads, rows, width = kvbuf.shape[1], kvbuf.shape[3], kvbuf.shape[4]
    wide = rows * group
    d = lax.axis_index("seq")
    x = lax.axis_index("kv")
    mesh_ids = pl.DeviceIdType.MESH

    partners = []
    step = 1
    while step < n_seq:
        up = lax.rem(lax.div(d, step), 2)
        partners.append((d + step - 2 * step * up, x))
        step *= 2
    step = 1
    while step < n_kv:
        up = lax.rem(lax.div(x, step), 2)
        partners.append((d, x + step - 2 * step * up))
        step *= 2

    barrier = pltpu.get_barrier_semaphore()
    for p in partners:
        pl.semaphore_signal(barrier, inc=1, device_id=p, device_id_type=mesh_ids)

    @pl.when(d > 0)
    def _():
        pl.semaphore_signal(barrier, inc=1, device_id=(d - 1, x), device_id_type=mesh_ids)

    @pl.when(d < n_seq - 1)
    def _():
        pl.semaphore_signal(barrier, inc=1, device_id=(d + 1, x), device_id_type=mesh_ids)

    @pl.when(d >= 4)
    def _():
        pl.semaphore_signal(barrier, inc=1, device_id=(d - 4, x), device_id_type=mesh_ids)

    @pl.when(d < n_seq - 4)
    def _():
        pl.semaphore_signal(barrier, inc=1, device_id=(d + 4, x), device_id_type=mesh_ids)

    def some(count):
        return lax.div(count + n_seq - 1, n_seq)

    after = n_seq - 1 - d
    peers = some(d) + some(after) + some(lax.div(d, 4)) + some(lax.div(after, 4))
    pl.semaphore_wait(barrier, len(partners) + peers)

    core = lax.rem(d, 2)
    high = lax.rem(lax.div(d, 2), 2)
    mate = d + 1 - 2 * core
    routes = [
        (0, 4, d + 4, d < n_seq - 4),
        (0, 2, d + 2, high == 0),
        (0, 1, d + 1, core == 0),
        (4, 3, d - 1, (core == 1) & (d >= 4)),
        (4, 2, d - 2, (high == 1) & (d >= 4)),
        (2, 3, d + 1, (core == 0) & (d >= 2)),
        (2, 1, d - 1, (core == 1) & (d >= 2)),
    ]

    def kv_copy(r, g):
        source, target, where, _ = routes[r]
        return pltpu.make_async_remote_copy(
            src_ref=kvbuf.at[source, g], dst_ref=kvbuf.at[target, g],
            send_sem=kv_send.at[r, g], recv_sem=kv_recv.at[target - 1, g],
            device_id=(where, x), device_id_type=mesh_ids,
        )

    def kv_start(r, g):
        @pl.when(routes[r][3])
        def _():
            kv_copy(r, g).start()

    def kv_wait(slot, g):
        pltpu.make_async_remote_copy(
            src_ref=kvbuf.at[0, g], dst_ref=kvbuf.at[slot, g],
            send_sem=kv_send.at[0, g], recv_sem=kv_recv.at[slot - 1, g],
            device_id=(mate, x), device_id_type=mesh_ids,
        ).wait_recv()

    def term_copy(i, g):
        return pltpu.make_async_remote_copy(
            src_ref=tbuf.at[i, g], dst_ref=rbuf.at[i, g],
            send_sem=t_send.at[i, g], recv_sem=t_recv.at[i, g],
            device_id=(d - 1, x), device_id_type=mesh_ids,
        )

    def term_sends(i):
        return d >= reach - i

    def term_arrives(i):
        return (d >= reach - i - 1) & (d < n_seq - 1)

    for k in range(1, blocks):
        @pl.when(d < k)
        def _():
            kvbuf[k] = jnp.zeros(kvbuf.shape[1:], bf16)

    @pl.when(d == n_seq - 1)
    def _():
        rbuf[reach - 1] = jnp.zeros(rbuf.shape[1:], bf16)

    part_scr[...] = jnp.zeros(part_scr.shape, f32)

    def prep(g):
        cols = pl.ds(pl.multiple_of(g * width, width), width)
        _, _, normed = normalize(k_ref[:, cols], kg_ref[...])
        rot = normed * cos_ref[...] + swap_halves(normed) * sin_ref[...]
        kvbuf[0, g, 0] = rot.astype(bf16)
        kvbuf[0, g, 1] = v_ref[:, cols]

    def attend(g):
        cos, sin, gain = cos_ref[...], sin_ref[...], qg_ref[...]
        cols = [
            pl.ds(pl.multiple_of((g * group + h) * width, width), width) for h in range(group)
        ]
        rots = []
        for h in range(group):
            _, _, normed = normalize(q_ref[:, cols[h]], gain)
            rots.append((normed * cos + swap_halves(normed) * sin).astype(bf16))
        q = jnp.concatenate(rots, axis=0)
        do = jnp.concatenate([do_ref[:, c] for c in cols], axis=0)
        low = low_ref[...]
        key_iota = lax.broadcasted_iota(jnp.int32, (rows, wide), 0)
        query_iota = lax.rem(lax.broadcasted_iota(jnp.int32, (1, wide), 1), rows)
        total = jnp.zeros((1, wide), f32)
        for j in range(blocks):
            s = dot(kvbuf[reach - j, g, 0], q, 1, 1)
            e = jnp.exp2(s * (attn_scale * log2_e))
            seen = key_iota >= low - j * rows
            if j == blocks - 1:
                seen = seen & (key_iota <= query_iota)
            e = jnp.where(seen, e, 0.0)
            total = total + jnp.sum(e, axis=0, keepdims=True)
            e_scr[j] = e
        inv_total = 1.0 / total
        delta = jnp.zeros((1, wide), f32)
        for j in range(blocks):
            w = e_scr[j] * inv_total
            wb = w.astype(bf16)
            gw = dot(kvbuf[reach - j, g, 1], do, 1, 1)
            delta = delta + jnp.sum(wb.astype(f32) * gw, axis=0, keepdims=True)
            gw_scr[j] = gw
            e_scr[j] = w
            term = dot(wb, do, 1, 0)
            if j < reach:
                tbuf[j, g, 1] = term.astype(bf16)
            else:
                own[g, 1] = term
        dq_t = jnp.zeros((width, wide), f32)
        for j in range(blocks):
            gs = (e_scr[j] * (gw_scr[j] - delta) * attn_scale).astype(bf16)
            dq_t = dq_t + dot(kvbuf[reach - j, g, 0], gs, 0, 0)
            term = dot(gs, q, 1, 0)
            if j < reach:
                tbuf[j, g, 0] = term.astype(bf16)
            else:
                own[g, 0] = term
        dq = dq_t.T
        for h in range(group):
            unit, inv, _ = normalize(q_ref[:, cols[h]], gain)
            out, p = norm_back(dq[h * rows : (h + 1) * rows], unit, inv, gain, cos, sin)
            dq_ref[:, cols[h]] = out.astype(bf16)
            part_scr[0] += p

    def finish(g):
        cols = pl.ds(pl.multiple_of(g * width, width), width)
        gain = kg_ref[...]
        unit, inv, _ = normalize(k_ref[:, cols], gain)
        dk = rbuf[reach - 1, g, 0].astype(f32) + own[g, 0]
        out, p = norm_back(dk, unit, inv, gain, cos_ref[...], sin_ref[...])
        dk_ref[:, cols] = out.astype(bf16)
        dv_ref[:, cols] = (rbuf[reach - 1, g, 1].astype(f32) + own[g, 1]).astype(bf16)
        part_scr[1] += p

    def turn(t, _):
        @pl.when(t < heads)
        def _():
            prep(t)

            for r in range(3):
                kv_start(r, t)

        g1 = t - 1

        @pl.when((g1 >= 0) & (g1 < heads))
        def _():
            @pl.when(d >= 4)
            def _():
                kv_wait(4, g1)
                kv_start(3, g1)
                kv_start(4, g1)

            @pl.when(high == 1)
            def _():
                kv_wait(2, g1)
                kv_start(5, g1)
                kv_start(6, g1)

        g2 = t - 2

        @pl.when((g2 >= 0) & (g2 < heads) & (high == 0) & (d >= 4))
        def _():
            kv_wait(2, g2)
            kv_start(5, g2)
            kv_start(6, g2)

        g = t - lag

        @pl.when((g >= 0) & (g < heads))
        def _():
            @pl.when(d >= 1)
            def _():
                kv_wait(1, g)

            @pl.when(d >= 3)
            def _():
                kv_wait(3, g)

            attend(g)

            @pl.when(term_sends(0))
            def _():
                term_copy(0, g).start()

        for i in range(1, reach):
            g = t - lag - i

            @pl.when((g >= 0) & (g < heads) & term_sends(i))
            def _():
                @pl.when(d < n_seq - 1)
                def _():
                    term_copy(i - 1, g).wait_recv()
                    tbuf[i, g] = (tbuf[i, g].astype(f32) + rbuf[i - 1, g].astype(f32)).astype(bf16)

                term_copy(i, g).start()

        f = t - lag - reach

        @pl.when((f >= 0) & (f < heads))
        def _():
            @pl.when(d < n_seq - 1)
            def _():
                term_copy(reach - 1, f).wait_recv()

            finish(f)

        return 0

    lax.fori_loop(0, heads + lag + reach, turn, 0)

    q_part = jnp.sum(part_scr[0], axis=0, keepdims=True)
    k_part = jnp.sum(part_scr[1], axis=0, keepdims=True)
    row = lax.broadcasted_iota(jnp.int32, (8, width), 0)
    total = jnp.where(row == 0, q_part, jnp.where(row == 1, k_part, 0.0))
    for r, p in enumerate(partners):
        gstage[r] = total
        copy = pltpu.make_async_remote_copy(
            src_ref=gstage.at[r], dst_ref=gbuf.at[r],
            send_sem=g_send.at[r], recv_sem=g_recv.at[r],
            device_id=p, device_id_type=mesh_ids,
        )
        copy.start()
        copy.wait()
        total = total + gbuf[r]
    gains_ref[...] = total

    def drain(g, _):
        for k in range(reach):
            @pl.when(term_sends(k))
            def _():
                term_copy(k, g).wait_send()

        for r in range(len(routes)):
            @pl.when(routes[r][3])
            def _():
                kv_copy(r, g).wait_send()

        return 0

    lax.fori_loop(0, heads, drain, 0)


def body(n_seq, n_kv, queries, keys, values, output_gradient, window_start, query_gain, key_gain):
    rows, q_heads, width = queries.shape
    kv_heads = keys.shape[1]
    group = q_heads // kv_heads
    reach = WINDOW_LENGTH // rows
    blocks = reach + 1
    first = lax.axis_index("seq") * rows
    cos, sin = rotary_tables(first + jnp.arange(rows, dtype=jnp.int32), width)
    low = jnp.tile(window_start - first + reach * rows, group)[None, :]
    q2 = queries.reshape(rows, q_heads * width)
    do2 = output_gradient.reshape(rows, q_heads * width)
    k2 = keys.reshape(rows, kv_heads * width)
    v2 = values.reshape(rows, kv_heads * width)
    rounds = (n_seq - 1).bit_length() + (n_kv - 1).bit_length()
    chunk = (kv_heads, 2, rows, width)
    dma = pltpu.SemaphoreType.DMA
    dq, dk, dv, gains = pl.pallas_call(
        functools.partial(fused_kernel, n_seq, n_kv, reach, group),
        out_shape=[
            jax.ShapeDtypeStruct(q2.shape, bf16),
            jax.ShapeDtypeStruct(k2.shape, bf16),
            jax.ShapeDtypeStruct(k2.shape, bf16),
            jax.ShapeDtypeStruct((8, width), f32),
        ],
        in_specs=[pl.BlockSpec(memory_space=pltpu.VMEM)] * 9,
        out_specs=[pl.BlockSpec(memory_space=pltpu.VMEM)] * 4,
        scratch_shapes=[
            pltpu.VMEM((blocks,) + chunk, bf16),
            pltpu.VMEM((reach,) + chunk, bf16),
            pltpu.VMEM((reach,) + chunk, bf16),
            pltpu.VMEM(chunk, f32),
            pltpu.VMEM((blocks, rows, rows * group), f32),
            pltpu.VMEM((blocks, rows, rows * group), f32),
            pltpu.VMEM((2, 8, width), f32),
            pltpu.VMEM((rounds, 8, width), f32),
            pltpu.VMEM((rounds, 8, width), f32),
        ]
        + [dma((7, kv_heads))]
        + [dma((reach, kv_heads))] * 3
        + [dma((rounds,))] * 2,
        compiler_params=pltpu.CompilerParams(
            collective_id=0, has_side_effects=True, vmem_limit_bytes=50 * 1024 * 1024
        ),
    )(q2, do2, k2, v2, low, query_gain[None, :], key_gain[None, :], cos, sin)
    return (
        dq.reshape(queries.shape),
        dk.reshape(keys.shape),
        dv.reshape(values.shape),
        gains[0],
        gains[1],
    )


def solution(mesh):
    split = P("seq", "kv", None)
    return jax.shard_map(
        functools.partial(body, mesh.shape["seq"], mesh.shape["kv"]),
        mesh=mesh,
        in_specs=(split, split, split, split, P("seq"), P(), P()),
        out_specs=(split, split, split, P(), P()),
        check_vma=False,
    )
```
